32 devices in a mesh: ctx: 8 (over y, x, core), ep: 4 (over z).
Axes of the slice: x: 2, y: 2, z: 4, core: 2. Of those that a mesh axis runs over, the one named last changes fastest.
Arguments:
- queries: bfloat16 [2048, 128, 192], P('ctx', 'ep'), may hold values from -7 to 7
- latents: bfloat16 [2048, 576], P('ctx'), may hold values from -7 to 7
- key_absorb: bfloat16 [128, 128, 512], P('ep'), may hold values from -0.5 to 0.5
- value_absorb: bfloat16 [128, 512, 128], P('ep'), may hold values from -1.5 to 1.5
- out_proj: bfloat16 [16384, 7168], P(None, 'ctx'), may hold values from -0.046875 to 0.046875
- residual_in: bfloat16 [2048, 7168], P(('ctx', 'ep')), may hold values from -3 to 3
- norm_gain: float32 [7168], replicated, may hold values from 0.1 to 1.9
- expert_gate: bfloat16 [4, 7168, 2048], P('ep', None, 'ctx'), may hold values from -0.0625 to 0.0625
- expert_up: bfloat16 [4, 7168, 2048], P('ep', None, 'ctx'), may hold values from -0.0625 to 0.0625
- expert_down: bfloat16 [4, 2048, 7168], P('ep', 'ctx'), may hold values from -0.125 to 0.125
- route_ids: int32 [2048, 8], P(('ctx', 'ep')), may hold values from 0 to 255, as said below
- route_weights: float32 [2048, 8], P(('ctx', 'ep')), may hold values from 0.5 to 1.5
Outputs:
- layer_out: bfloat16 [2048, 7168], P(('ctx', 'ep'))
The draws below stay inside these ranges and needn't reach their ends.
Inputs may be any that keep to these rules, and one draw needn't show every extreme that they name: `route_ids`: each row names 8 different experts. In every aligned block of 64 rows (the rows of one device) each expert below 4 is named by at most 2 rows, and some expert by exactly 2.
All inputs are finite; a program needn't handle non-finite values.
Results may differ from the reference program's by a relative error of at most 0.028.
Values may be sent and summed in bfloat16 or wider, within the bound.
A program may use at most 320 MiB of HBM per device.

```python
import jax
import jax.numpy as jnp
from jax import lax

D = 7168
HEADS = 128
NOPE = 128
ROPE = 64
LATENT = 512
VHEAD = 128
FF = 2048
EXPERTS = 256
TOPK = 8
CAP = 2
CONTEXT = 2048
TOK_MOE = 64
WINDOW_EXPERTS = 4


def draw_latents(key, part):
    key = jax.random.fold_in(key, 3)
    values = jnp.clip(jax.random.normal(key, (CONTEXT, LATENT + ROPE), jnp.float32), -7.0, 7.0)
    return values.astype(jnp.bfloat16)


def draw_queries(key, part):
    key = jax.random.fold_in(key, 5)
    shape = (CONTEXT, HEADS, NOPE + ROPE)
    values = jnp.clip(jax.random.normal(key, shape, jnp.float32), -7.0, 7.0)
    return values.astype(jnp.bfloat16)


def draw_route_ids(key, part):
    key = jax.random.fold_in(key, 11)
    blocks = CONTEXT // TOK_MOE
    window = WINDOW_EXPERTS
    keys = jax.random.split(key, 6)
    limits = jax.random.randint(keys[0], (window,), 1, 2 * CAP + 1, dtype=jnp.int32)
    counts = jax.random.randint(keys[1], (blocks, window), 0, 2 * CAP + 1, dtype=jnp.int32)
    counts = jnp.minimum(jnp.minimum(counts, limits[None, :]), CAP)
    forced = jax.random.randint(keys[2], (blocks,), 0, window, dtype=jnp.int32)
    counts = jnp.where(jnp.arange(window, dtype=jnp.int32)[None, :] == forced[:, None], CAP, counts)
    ranking = jax.random.randint(keys[3], (blocks, window, TOK_MOE), 0, 2 ** 16, dtype=jnp.int32) * TOK_MOE + jnp.arange(TOK_MOE, dtype=jnp.int32)
    order = jnp.argsort(ranking, axis=-1)
    ranks = jnp.argsort(order, axis=-1).astype(jnp.int32)
    member = jnp.transpose(ranks < counts[:, :, None], (0, 2, 1))
    member_int = member.astype(jnp.int32)
    position = jnp.cumsum(member_int, axis=-1).astype(jnp.int32) - 1
    matches = member[:, :, None, :] & (position[:, :, None, :] == jnp.arange(TOPK, dtype=jnp.int32)[None, None, :, None])
    window_list = jnp.sum(jnp.arange(window, dtype=jnp.int32)[None, None, None, :] * matches.astype(jnp.int32), axis=-1)
    taken = jnp.sum(member_int, axis=-1)
    rest = EXPERTS - window
    other_scores = jax.random.randint(keys[4], (blocks, TOK_MOE, rest), 0, 2 ** 16, dtype=jnp.int32) * rest + jnp.arange(rest, dtype=jnp.int32)
    others = lax.top_k(other_scores, TOPK)[1].astype(jnp.int32) + window
    rows = jnp.where(jnp.arange(TOPK, dtype=jnp.int32)[None, None, :] < taken[:, :, None], window_list, others)
    shuffle = jax.random.randint(keys[5], (blocks, TOK_MOE, TOPK), 0, 2 ** 16, dtype=jnp.int32) * TOPK + jnp.arange(TOPK, dtype=jnp.int32)
    rows = jnp.take_along_axis(rows, jnp.argsort(shuffle, axis=-1), axis=-1)
    return rows.reshape(CONTEXT, TOPK).astype(jnp.int32)


def shard_levels(stream_key, dims, cuts, smallest, top_value):
    def one(axis_at, parts):
        steps = jax.random.uniform(jax.random.fold_in(jax.random.fold_in(stream_key, 6), axis_at), (parts,), jnp.float32, smallest / len(cuts), top_value / len(cuts))
        return jnp.repeat(jnp.exp(steps), dims[axis_at] // parts).reshape((-1,) + (1,) * (len(dims) - axis_at - 1))

    factor_of = one(*cuts[0])
    for cut in cuts[1:]:
        factor_of = factor_of * one(*cut)
    return factor_of


def bell_draw(stream_key, extent, scale, bound, shards=(), held_as=jnp.bfloat16):
    gain = shard_levels(stream_key, extent, shards, -0.22, 0.18) if shards else 1.0
    result = jax.random.normal(stream_key, extent, jnp.float32) * scale * gain
    return jnp.minimum(jnp.maximum(result, -bound), bound).astype(held_as)


def setup_inputs(seed: int = 0) -> dict:
    key_list = jax.random.split(jax.random.key(seed), 13)
    queries = draw_queries(jax.random.fold_in(key_list[12], 71), 0)
    latents = draw_latents(jax.random.fold_in(key_list[12], 71), 0)
    key_absorb = bell_draw(key_list[2], (HEADS, NOPE, LATENT), NOPE ** -0.5, 0.5, ((0, 4),))
    value_absorb = bell_draw(key_list[3], (HEADS, LATENT, VHEAD), 0.25, 1.5, ((0, 4),))
    out_proj = bell_draw(key_list[4], (HEADS * VHEAD, D), (HEADS * VHEAD) ** -0.5, 0.046875, ((1, 8),))
    residual_in = bell_draw(key_list[5], (CONTEXT, D), 0.5, 3.0, ((0, 32),))
    norm_gain = jnp.clip(1.0 + 0.18 * jax.random.normal(key_list[6], (D,), jnp.float32), 0.1, 1.9)
    expert_gate = bell_draw(key_list[7], (WINDOW_EXPERTS, D, FF), D ** -0.5, 0.0625, ((0, 4), (2, 8)))
    expert_up = bell_draw(key_list[8], (WINDOW_EXPERTS, D, FF), D ** -0.5, 0.0625, ((0, 4), (2, 8)))
    expert_down = bell_draw(key_list[9], (WINDOW_EXPERTS, FF, D), FF ** -0.5, 0.125, ((0, 4), (1, 8)))
    route_ids = draw_route_ids(jax.random.fold_in(key_list[12], 71), 0)
    route_weights = jnp.clip(0.5 + 1.0 * jax.random.uniform(key_list[11], (CONTEXT, TOPK), jnp.float32) ** shard_levels(key_list[11], (CONTEXT, TOPK), ((0, 32),), -0.2, 0.2), 0.5, 1.5)
    return dict(queries=queries, latents=latents, key_absorb=key_absorb, value_absorb=value_absorb, out_proj=out_proj, residual_in=residual_in, norm_gain=norm_gain, expert_gate=expert_gate, expert_up=expert_up, expert_down=expert_down, route_ids=route_ids, route_weights=route_weights)


def head_output(query_nope, query_rope, absorb_key, absorb_value, latents):
    absorbed = jnp.dot(query_nope, absorb_key, preferred_element_type=jnp.float32).astype(jnp.bfloat16)
    query_full = jnp.concatenate([absorbed, query_rope], axis=1)
    scale = (NOPE + ROPE) ** (-0.5)
    compressed = latents[:, :LATENT]
    pieces = []
    for begin in range(0, CONTEXT, 512):
        finish = min(begin + 512, CONTEXT)
        scores = jnp.dot(query_full[begin:finish], latents[:finish].T, preferred_element_type=jnp.float32) * scale
        allowed = jnp.arange(begin, finish)[:, None] >= jnp.arange(finish)[None, :]
        scores = jnp.where(allowed, scores, -jnp.inf)
        probs = jax.nn.softmax(scores, axis=1).astype(jnp.bfloat16)
        mixed = jnp.dot(probs, compressed[:finish], preferred_element_type=jnp.float32).astype(jnp.bfloat16)
        pieces.append(jnp.dot(mixed, absorb_value, preferred_element_type=jnp.float32).astype(jnp.bfloat16))
    return jnp.concatenate(pieces, axis=0)

def reference(queries, latents, key_absorb, value_absorb, out_proj, residual_in, norm_gain, expert_gate, expert_up, expert_down, route_ids, route_weights):
    by_head = jnp.transpose(queries, (1, 0, 2))

    def one_head(packed):
        head_queries, absorb_key, absorb_value = packed
        return head_output(head_queries[:, :NOPE], head_queries[:, NOPE:], absorb_key, absorb_value, latents)
    heads = lax.map(one_head, (by_head, key_absorb, value_absorb))
    flat = jnp.transpose(heads, (1, 0, 2)).reshape(CONTEXT, HEADS * VHEAD)
    attended = jnp.dot(flat, out_proj, preferred_element_type=jnp.float32).astype(jnp.bfloat16)
    attended = lax.optimization_barrier(attended)
    hidden = (residual_in.astype(jnp.float32) + attended.astype(jnp.float32)).astype(jnp.bfloat16)
    hidden = lax.optimization_barrier(hidden)
    wide = hidden.astype(jnp.float32)
    square = lax.optimization_barrier(jnp.mean(wide * wide, axis=1, keepdims=True))
    normed = (wide * lax.rsqrt(square + 1e-06) * norm_gain.astype(jnp.float32)).astype(jnp.bfloat16)
    normed = lax.optimization_barrier(normed)
    blocks = CONTEXT // TOK_MOE
    flat_ids = route_ids.reshape(blocks, TOK_MOE * TOPK).astype(jnp.int32)
    chosen = (flat_ids[:, :, None] == jnp.arange(WINDOW_EXPERTS, dtype=jnp.int32)[None, None, :]).astype(jnp.int32)
    earlier = jnp.cumsum(chosen, axis=1).astype(jnp.int32) - chosen
    slot = lax.optimization_barrier(jnp.sum(earlier * chosen, axis=2)).astype(jnp.int32)
    place = chosen[:, :, :, None] * (slot[:, :, None, None] == jnp.arange(CAP, dtype=jnp.int32)[None, None, None, :]).astype(jnp.int32)
    place = place.reshape(blocks, TOK_MOE, TOPK, WINDOW_EXPERTS, CAP).astype(jnp.float32)
    gather_table = lax.optimization_barrier(jnp.sum(place, axis=2))
    tokens = normed.reshape(blocks, TOK_MOE, D).astype(jnp.float32)
    sent = jnp.einsum('btwc,btd->wbcd', gather_table, tokens).astype(jnp.bfloat16)

    def run_expert(packed):
        rows, gate_weight, up_weight, down_weight = packed
        flat_rows = rows.reshape(blocks * CAP, D)
        gate = jnp.dot(flat_rows, gate_weight, preferred_element_type=jnp.float32)
        upper = jnp.dot(flat_rows, up_weight, preferred_element_type=jnp.float32)
        activated = (jax.nn.silu(gate) * upper).astype(jnp.bfloat16)
        return jnp.dot(activated, down_weight, preferred_element_type=jnp.float32).astype(jnp.bfloat16).reshape(blocks, CAP, D)
    outputs = lax.map(run_expert, (sent, expert_gate, expert_up, expert_down))
    outputs = lax.optimization_barrier(outputs)
    weights = route_weights.reshape(blocks, TOK_MOE, TOPK).astype(jnp.float32)
    combine_table = lax.optimization_barrier(jnp.sum(place * weights[:, :, :, None, None], axis=2))
    mixture = jnp.einsum('btwc,wbcd->btd', combine_table, outputs.astype(jnp.float32), precision=lax.Precision.HIGHEST)
    return (wide + mixture.reshape(CONTEXT, D)).astype(jnp.bfloat16)
```

```python
import jax
import jax.numpy as jnp
from jax import lax
from jax.experimental import pallas as pl
from jax.experimental.pallas import tpu as pltpu
from jax.sharding import PartitionSpec as P

NOPE = 128
ROPE = 64
LATENT = 512
VHEAD = 128
TOPK = 8
CAP = 2
CHUNKS = 4
KEY_BLOCK = 512
LOG2E = 1.4426950408889634


def over_first(a, b):
    return lax.dot_general(a, b, (((0,), (0,)), ((), ())), preferred_element_type=jnp.float32)


def attention_kernel(start_ref, q_ref, ka_ref, va_ref, lat_ref, latt_ref, out_ref, qf_ref, s_ref):
    factor = (NOPE + ROPE) ** (-0.5) * LOG2E
    rows = q_ref.shape[2]
    keys = lat_ref.shape[0]
    query_start = start_ref[0]
    absorbed = over_first(ka_ref[0], q_ref[0, :NOPE, :])
    qf_ref[:LATENT, :] = (absorbed * factor).astype(jnp.bfloat16)
    qf_ref[LATENT:, :] = (q_ref[0, NOPE:, :].astype(jnp.float32) * factor).astype(jnp.bfloat16)
    ahead = lax.broadcasted_iota(jnp.int32, (KEY_BLOCK, rows), 0) - lax.broadcasted_iota(
        jnp.int32, (KEY_BLOCK, rows), 1
    )
    top = jnp.full((8, rows), -1e30, jnp.float32)
    for begin in range(0, keys, KEY_BLOCK):
        scores = jnp.dot(
            lat_ref[begin : begin + KEY_BLOCK, :], qf_ref[...], preferred_element_type=jnp.float32
        )
        scores = jnp.where(ahead <= query_start - begin, scores, -1e30)
        s_ref[begin : begin + KEY_BLOCK, :] = scores
        top = jnp.maximum(top, jnp.max(scores.reshape(KEY_BLOCK // 8, 8, rows), axis=0))
    top = jnp.max(top, axis=0, keepdims=True)
    total = jnp.zeros((8, rows), jnp.float32)
    mixed = jnp.zeros((LATENT, rows), jnp.float32)
    for begin in range(0, keys, KEY_BLOCK):
        weights = jnp.exp2(s_ref[begin : begin + KEY_BLOCK, :] - top)
        total = total + jnp.sum(weights.reshape(KEY_BLOCK // 8, 8, rows), axis=0)
        mixed = mixed + jnp.dot(
            latt_ref[:LATENT, begin : begin + KEY_BLOCK],
            weights.astype(jnp.bfloat16),
            preferred_element_type=jnp.float32,
        )
    inverse = 1.0 / jnp.sum(total, axis=0, keepdims=True)
    mixed = (mixed * inverse).astype(jnp.bfloat16)
    out_ref[...] = over_first(mixed, va_ref[0]).astype(jnp.bfloat16)


def attention(chunk, count, query_start, queries_t, key_absorb, value_absorb, keys, keys_t):
    rows = queries_t.shape[2]
    width = queries_t.shape[1]
    total, latent_width = keys.shape
    first = chunk * count

    def by_head(i, _):
        return (first + i, 0, 0)

    return pl.pallas_call(
        attention_kernel,
        grid_spec=pltpu.PrefetchScalarGridSpec(
            num_scalar_prefetch=1,
            grid=(count,),
            in_specs=[
                pl.BlockSpec((1, width, rows), by_head),
                pl.BlockSpec((1, NOPE, LATENT), by_head),
                pl.BlockSpec((1, LATENT, VHEAD), by_head),
                pl.BlockSpec((total, latent_width), lambda i, _: (0, 0)),
                pl.BlockSpec((latent_width, total), lambda i, _: (0, 0)),
            ],
            out_specs=pl.BlockSpec((rows, VHEAD), lambda i, _: (0, i)),
            scratch_shapes=[
                pltpu.VMEM((latent_width, rows), jnp.bfloat16),
                pltpu.VMEM((total, rows), jnp.float32),
            ],
        ),
        out_shape=jax.ShapeDtypeStruct((rows, count * VHEAD), jnp.bfloat16),
        compiler_params=pltpu.CompilerParams(vmem_limit_bytes=48 * 2 ** 20),
        cost_estimate=pl.CostEstimate(
            flops=4 * count * rows * total * (latent_width + LATENT),
            bytes_accessed=count * (rows * 320 + 2 * NOPE * LATENT) * 2 + 4 * total * latent_width,
            transcendentals=count * rows * total,
        ),
    )(query_start, queries_t, key_absorb, value_absorb, keys, keys_t)


def on_device(
    queries,
    latents,
    key_absorb,
    value_absorb,
    out_proj,
    residual_in,
    norm_gain,
    expert_gate,
    expert_up,
    expert_down,
    route_ids,
    route_weights,
):
    rows = queries.shape[0]
    local_heads = queries.shape[1]
    columns = out_proj.shape[1]
    ctx_count = lax.axis_size("ctx")
    ep_count = lax.axis_size("ep")
    ep_me = lax.axis_index("ep")
    owned = rows // ep_count
    query_start = (lax.axis_index("ctx") * rows).astype(jnp.int32).reshape(1)

    keys = lax.all_gather(latents, "ctx", axis=0, tiled=True)
    keys_t = keys.T
    queries_t = jnp.transpose(queries, (1, 2, 0))

    count = local_heads // CHUNKS
    depth = count * VHEAD
    complete = jnp.zeros((ctx_count * owned, columns), jnp.float32)
    before = None
    for chunk in range(CHUNKS):
        heads = attention(
            chunk, count, query_start, queries_t, key_absorb, value_absorb, keys, keys_t
        )
        pieces = [lax.dynamic_slice_in_dim(heads, ep_me * owned, owned, axis=0)]
        for shift in range(1, ep_count):
            target = lax.rem(ep_me + shift, ep_count)
            block = lax.dynamic_slice_in_dim(heads, target * owned, owned, axis=0)
            pieces.append(
                lax.ppermute(
                    block, "ep", [(i, (i + shift) % ep_count) for i in range(ep_count)]
                )
            )
        mine = jnp.concatenate(pieces, axis=1)
        if before is not None:
            mine, before = lax.optimization_barrier((mine, before))
        gathered = lax.all_gather(mine, "ctx", axis=0, tiled=True)
        before = gathered[:8, :128]
        for shift in range(ep_count):
            source = lax.rem(ep_me - shift + ep_count, ep_count)
            weight = lax.dynamic_slice_in_dim(
                out_proj, source * (local_heads * VHEAD) + chunk * depth, depth, axis=0
            )
            complete = complete + jnp.dot(
                gathered[:, shift * depth : (shift + 1) * depth],
                weight,
                preferred_element_type=jnp.float32,
            )
    complete = complete.astype(jnp.bfloat16).reshape(ctx_count, -1, columns)
    attended = lax.all_to_all(complete, "ctx", split_axis=0, concat_axis=2, tiled=True).reshape(
        -1, columns * ctx_count
    )
    wide = residual_in.astype(jnp.float32) + attended.astype(jnp.float32)
    hidden = wide.astype(jnp.bfloat16)
    hidden_wide = hidden.astype(jnp.float32)
    square = jnp.mean(hidden_wide * hidden_wide, axis=1, keepdims=True)
    normed = (hidden_wide * lax.rsqrt(square + 1e-06) * norm_gain).astype(jnp.bfloat16)
    tokens_here = hidden.shape[0]
    window = ep_count
    flat_ids = route_ids.reshape(-1)
    chosen = (flat_ids[:, None] == jnp.arange(window, dtype=jnp.int32)[None, :]).astype(jnp.int32)
    earlier = jnp.cumsum(chosen, axis=0) - chosen
    slot = jnp.sum(earlier * chosen, axis=1)
    place = chosen[:, :, None] * (
        slot[:, None, None] == jnp.arange(CAP, dtype=jnp.int32)[None, None, :]
    ).astype(jnp.int32)
    place = place.reshape(tokens_here, TOPK, window * CAP).astype(jnp.float32)
    gather_table = jnp.sum(place, axis=1).astype(jnp.bfloat16)
    combine_table = jnp.sum(place * route_weights[:, :, None], axis=1)
    outgoing = lax.dot_general(
        gather_table, normed, (((0,), (0,)), ((), ())), preferred_element_type=jnp.float32
    ).astype(jnp.bfloat16)
    outgoing = outgoing.reshape(window, CAP, -1)
    arrived = lax.all_to_all(outgoing, "ep", split_axis=0, concat_axis=0, tiled=True)
    gate_weight = expert_gate[0]
    up_weight = expert_up[0]
    down_weight = expert_down[0]

    flat_rows = lax.all_gather(arrived, "ctx", axis=0, tiled=True).reshape(
        ctx_count * window * CAP, -1
    )
    gate = jnp.dot(flat_rows, gate_weight, preferred_element_type=jnp.float32)
    upper = jnp.dot(flat_rows, up_weight, preferred_element_type=jnp.float32)
    activated = (jax.nn.silu(gate) * upper).astype(jnp.bfloat16)
    partial_out = jnp.dot(activated, down_weight, preferred_element_type=jnp.float32)
    partial_out = partial_out.astype(jnp.bfloat16).reshape(ctx_count, window * CAP, -1)
    parts = lax.all_to_all(partial_out, "ctx", split_axis=0, concat_axis=0, tiled=True)
    result = jnp.sum(parts.astype(jnp.float32), axis=0).astype(jnp.bfloat16)
    result = result.reshape(window, CAP, -1)
    returned = lax.all_to_all(result, "ep", split_axis=0, concat_axis=0, tiled=True)
    mixture = jnp.dot(
        combine_table,
        returned.reshape(window * CAP, -1).astype(jnp.float32),
        precision=lax.Precision.HIGHEST,
    )
    return (hidden_wide + mixture).astype(jnp.bfloat16)


def solution(mesh):
    placed = (
        P("ctx", "ep", None),
        P("ctx", None),
        P("ep", None, None),
        P("ep", None, None),
        P(None, "ctx"),
        P(("ctx", "ep"), None),
        P(),
        P("ep", None, "ctx"),
        P("ep", None, "ctx"),
        P("ep", "ctx", None),
        P(("ctx", "ep"), None),
        P(("ctx", "ep"), None),
    )
    return jax.shard_map(
        on_device, mesh=mesh, in_specs=placed, out_specs=P(("ctx", "ep"), None), check_vma=False
    )
```

```python
import functools

import jax
import jax.numpy as jnp
from jax import lax
from jax.experimental import pallas as pl
from jax.experimental.pallas import tpu as pltpu
from jax.sharding import PartitionSpec as P

NOPE = 128
ROPE = 64
LATENT = 512
VHEAD = 128
TOPK = 8
CAP = 2
CHUNKS = 4
KEY_BLOCK = 256
GROUP = 4
LOG2E = 1.4426950408889634


def over_first(a, b):
    return lax.dot_general(a, b, (((0,), (0,)), ((), ())), preferred_element_type=jnp.float32)


def attention_kernel(
    start_ref, q_ref, ka_ref, va_ref, lat_ref, latt_ref, out_ref, qf_ref, even_ref, odd_ref
):
    factor = (NOPE + ROPE) ** (-0.5) * LOG2E
    group, _, rows = q_ref.shape
    keys = lat_ref.shape[0]
    query_start = start_ref[0]
    slots = (even_ref, odd_ref)
    ahead = lax.broadcasted_iota(jnp.int32, (KEY_BLOCK, rows), 0) - lax.broadcasted_iota(
        jnp.int32, (KEY_BLOCK, rows), 1
    )
    for head in range(group):
        absorbed = over_first(ka_ref[head], q_ref[head, :NOPE, :])
        qf_ref[head, :LATENT, :] = (absorbed * factor).astype(jnp.bfloat16)
        qf_ref[head, LATENT:, :] = (q_ref[head, NOPE:, :].astype(jnp.float32) * factor).astype(
            jnp.bfloat16
        )

    highest = None
    for step in range(group + 1):
        top = jnp.full((8, rows), -1e30, jnp.float32)
        total = jnp.zeros((8, rows), jnp.float32)
        mixed = jnp.zeros((LATENT, rows), jnp.float32)
        for begin in range(0, keys, KEY_BLOCK):
            block = pl.ds(begin, KEY_BLOCK)
            if step < group:
                scores = jnp.dot(
                    lat_ref[block, :], qf_ref[step], preferred_element_type=jnp.float32
                )
                scores = jnp.where(ahead <= query_start - begin, scores, -1e30)
                slots[step % 2][block, :] = scores
                top = jnp.maximum(top, jnp.max(scores.reshape(KEY_BLOCK // 8, 8, rows), axis=0))
            if step > 0:
                weights = jnp.exp2(slots[(step - 1) % 2][block, :] - highest)
                total = total + jnp.sum(weights.reshape(KEY_BLOCK // 8, 8, rows), axis=0)
                mixed = mixed + jnp.dot(
                    latt_ref[:LATENT, block],
                    weights.astype(jnp.bfloat16),
                    preferred_element_type=jnp.float32,
                )
        if step > 0:
            inverse = 1.0 / jnp.sum(total, axis=0, keepdims=True)
            out_ref[:, pl.ds((step - 1) * VHEAD, VHEAD)] = over_first(
                (mixed * inverse).astype(jnp.bfloat16), va_ref[step - 1]
            ).astype(jnp.bfloat16)
        highest = jnp.max(top, axis=0, keepdims=True)


def attention(chunk, count, query_start, queries_t, key_absorb, value_absorb, keys, keys_t):
    _, width, rows = queries_t.shape
    total, latent_width = keys.shape
    group = GROUP if count % GROUP == 0 else 1
    first = chunk * count // group

    def by_head(i, _):
        return (first + i, 0, 0)

    return pl.pallas_call(
        attention_kernel,
        grid_spec=pltpu.PrefetchScalarGridSpec(
            num_scalar_prefetch=1,
            grid=(count // group,),
            in_specs=[
                pl.BlockSpec((group, width, rows), by_head),
                pl.BlockSpec((group, NOPE, LATENT), by_head),
                pl.BlockSpec((group, LATENT, VHEAD), by_head),
                pl.BlockSpec((total, latent_width), lambda i, _: (0, 0)),
                pl.BlockSpec((latent_width, total), lambda i, _: (0, 0)),
            ],
            out_specs=pl.BlockSpec((rows, group * VHEAD), lambda i, _: (0, i)),
            scratch_shapes=[
                pltpu.VMEM((group, latent_width, rows), jnp.bfloat16),
                pltpu.VMEM((total, rows), jnp.float32),
                pltpu.VMEM((total, rows), jnp.float32),
            ],
        ),
        out_shape=jax.ShapeDtypeStruct((rows, count * VHEAD), jnp.bfloat16),
        compiler_params=pltpu.CompilerParams(vmem_limit_bytes=50 * 2 ** 20),
        cost_estimate=pl.CostEstimate(
            flops=4 * count * rows * total * (latent_width + LATENT),
            bytes_accessed=count * (rows * 320 + 2 * NOPE * LATENT) * 2 + 4 * total * latent_width,
            transcendentals=count * rows * total,
        ),
    )(query_start, queries_t, key_absorb, value_absorb, keys, keys_t)


def join_kernel(count, *refs):
    width = refs[0].shape[1]
    for place in range(count):
        refs[-1][:, pl.ds(place * width, width)] = refs[place][...]


def join(pieces, after):
    rows, width = pieces[0].shape
    later = [] if after is None else [after]
    return pl.pallas_call(
        functools.partial(join_kernel, len(pieces)),
        in_specs=[pl.BlockSpec(memory_space=pltpu.VMEM)] * len(pieces)
        + [pl.BlockSpec(memory_space=pl.ANY)] * len(later),
        out_specs=pl.BlockSpec(memory_space=pltpu.VMEM),
        out_shape=jax.ShapeDtypeStruct((rows, width * len(pieces)), jnp.bfloat16),
    )(*pieces, *later)


def project_kernel(added, source_ref, *refs):
    rows_ref, weight_ref, out_ref, sum_ref = refs[added:]
    step = pl.program_id(0)
    product = jnp.dot(rows_ref[...], weight_ref[...], preferred_element_type=jnp.float32)

    @pl.when(step == 0)
    def _():
        sum_ref[...] = product + refs[0][...] if added else product

    @pl.when(step > 0)
    def _():
        sum_ref[...] += product

    @pl.when(step == pl.num_programs(0) - 1)
    def _():
        out_ref[...] = sum_ref[...].astype(out_ref.dtype)


def project(so_far, gathered, out_proj, blocks, depth, held_as):
    rows, columns = gathered.shape[0], out_proj.shape[1]
    added = so_far is not None
    whole = pl.BlockSpec((rows, columns), lambda i, _: (0, 0))
    return pl.pallas_call(
        functools.partial(project_kernel, int(added)),
        grid_spec=pltpu.PrefetchScalarGridSpec(
            num_scalar_prefetch=1,
            grid=(gathered.shape[1] // depth,),
            in_specs=[whole] * added
            + [
                pl.BlockSpec((rows, depth), lambda i, _: (0, i)),
                pl.BlockSpec((depth, columns), lambda i, blocks: (blocks[i], 0)),
            ],
            out_specs=whole,
            scratch_shapes=[pltpu.VMEM((rows, columns), jnp.float32)],
        ),
        out_shape=jax.ShapeDtypeStruct((rows, columns), held_as),
        compiler_params=pltpu.CompilerParams(vmem_limit_bytes=40 * 2 ** 20),
        cost_estimate=pl.CostEstimate(
            flops=2 * rows * gathered.shape[1] * columns,
            bytes_accessed=2 * gathered.shape[1] * (rows + columns) + 8 * rows * columns,
            transcendentals=0,
        ),
    )(blocks, *([so_far] * added), gathered, out_proj)


def on_device(
    queries,
    latents,
    key_absorb,
    value_absorb,
    out_proj,
    residual_in,
    norm_gain,
    expert_gate,
    expert_up,
    expert_down,
    route_ids,
    route_weights,
):
    rows = queries.shape[0]
    local_heads = queries.shape[1]
    columns = out_proj.shape[1]
    ctx_count = lax.axis_size("ctx")
    ep_count = lax.axis_size("ep")
    ep_me = lax.axis_index("ep")
    owned = rows // ep_count
    query_start = (lax.axis_index("ctx") * rows).astype(jnp.int32).reshape(1)

    keys = lax.all_gather(latents, "ctx", axis=0, tiled=True)
    keys_t = keys.T
    queries_t = jnp.transpose(queries, (1, 2, 0))

    count = local_heads // CHUNKS
    depth = count * VHEAD
    sources = lax.rem(ep_me + ep_count - jnp.arange(ep_count, dtype=jnp.int32), ep_count)
    heads = [
        attention(chunk, count, query_start, queries_t, key_absorb, value_absorb, keys, keys_t)
        for chunk in range(CHUNKS)
    ]
    complete = None
    for chunk in range(CHUNKS):
        pieces = [lax.dynamic_slice_in_dim(heads[chunk], ep_me * owned, owned, axis=0)]
        for shift in range(1, ep_count):
            target = lax.rem(ep_me + shift, ep_count)
            block = lax.dynamic_slice_in_dim(heads[chunk], target * owned, owned, axis=0)
            pieces.append(
                lax.ppermute(
                    block, "ep", [(i, (i + shift) % ep_count) for i in range(ep_count)]
                )
            )
        last = chunk == CHUNKS - 1
        mine = join(pieces, None if last else heads[chunk + 1])
        gathered = lax.all_gather(mine, "ctx", axis=0, tiled=True)
        complete = project(
            complete,
            gathered,
            out_proj,
            sources * CHUNKS + chunk,
            depth,
            jnp.bfloat16 if last else jnp.float32,
        )
    complete = complete.reshape(ctx_count, -1, columns)
    attended = lax.all_to_all(complete, "ctx", split_axis=0, concat_axis=2, tiled=True).reshape(
        -1, columns * ctx_count
    )
    wide = residual_in.astype(jnp.float32) + attended.astype(jnp.float32)
    hidden = wide.astype(jnp.bfloat16)
    hidden_wide = hidden.astype(jnp.float32)
    square = jnp.mean(hidden_wide * hidden_wide, axis=1, keepdims=True)
    normed = (hidden_wide * lax.rsqrt(square + 1e-06) * norm_gain).astype(jnp.bfloat16)
    tokens_here = hidden.shape[0]
    window = ep_count
    flat_ids = route_ids.reshape(-1)
    chosen = (flat_ids[:, None] == jnp.arange(window, dtype=jnp.int32)[None, :]).astype(jnp.int32)
    earlier = jnp.cumsum(chosen, axis=0) - chosen
    slot = jnp.sum(earlier * chosen, axis=1)
    place = chosen[:, :, None] * (
        slot[:, None, None] == jnp.arange(CAP, dtype=jnp.int32)[None, None, :]
    ).astype(jnp.int32)
    place = place.reshape(tokens_here, TOPK, window * CAP).astype(jnp.float32)
    gather_table = jnp.sum(place, axis=1).astype(jnp.bfloat16)
    combine_table = jnp.sum(place * route_weights[:, :, None], axis=1)
    outgoing = lax.dot_general(
        gather_table, normed, (((0,), (0,)), ((), ())), preferred_element_type=jnp.float32
    ).astype(jnp.bfloat16)
    outgoing = outgoing.reshape(window, CAP, -1)
    arrived = lax.all_to_all(outgoing, "ep", split_axis=0, concat_axis=0, tiled=True)
    gate_weight = expert_gate[0]
    up_weight = expert_up[0]
    down_weight = expert_down[0]

    flat_rows = lax.all_gather(arrived, "ctx", axis=0, tiled=True).reshape(
        ctx_count * window * CAP, -1
    )
    gate = jnp.dot(flat_rows, gate_weight, preferred_element_type=jnp.float32)
    upper = jnp.dot(flat_rows, up_weight, preferred_element_type=jnp.float32)
    activated = (jax.nn.silu(gate) * upper).astype(jnp.bfloat16)
    partial_out = jnp.dot(activated, down_weight, preferred_element_type=jnp.float32)
    partial_out = partial_out.astype(jnp.bfloat16).reshape(ctx_count, window * CAP, -1)
    parts = lax.all_to_all(partial_out, "ctx", split_axis=0, concat_axis=0, tiled=True)
    result = jnp.sum(parts.astype(jnp.float32), axis=0).astype(jnp.bfloat16)
    result = result.reshape(window, CAP, -1)
    returned = lax.all_to_all(result, "ep", split_axis=0, concat_axis=0, tiled=True)
    mixture = jnp.dot(
        combine_table,
        returned.reshape(window * CAP, -1).astype(jnp.float32),
        precision=lax.Precision.HIGHEST,
    )
    return (hidden_wide + mixture).astype(jnp.bfloat16)


def solution(mesh):
    placed = (
        P("ctx", "ep", None),
        P("ctx", None),
        P("ep", None, None),
        P("ep", None, None),
        P(None, "ctx"),
        P(("ctx", "ep"), None),
        P(),
        P("ep", None, "ctx"),
        P("ep", None, "ctx"),
        P("ep", "ctx", None),
        P(("ctx", "ep"), None),
        P(("ctx", "ep"), None),
    )
    return jax.shard_map(
        on_device, mesh=mesh, in_specs=placed, out_specs=P(("ctx", "ep"), None), check_vma=False
    )
```

```python
import functools

import jax
import jax.numpy as jnp
from jax import lax
from jax.experimental import pallas as pl
from jax.experimental.pallas import tpu as pltpu
from jax.sharding import PartitionSpec as P

NOPE = 128
ROPE = 64
LATENT = 512
VHEAD = 128
TOPK = 8
CAP = 2
EIGHTHS = (3, 1, 4)
KEY_BLOCK = 256
LOG2E = 1.4426950408889634


def over_first(a, b):
    return lax.dot_general(a, b, (((0,), (0,)), ((), ())), preferred_element_type=jnp.float32)


def attention_kernel(
    start_ref, q_ref, ka_ref, va_ref, lat_ref, latt_ref, out_ref, qf_ref, even_ref, odd_ref
):
    factor = (NOPE + ROPE) ** (-0.5) * LOG2E
    group, _, rows = q_ref.shape
    keys = lat_ref.shape[0]
    query_start = start_ref[0]
    slots = (even_ref, odd_ref)
    ahead = lax.broadcasted_iota(jnp.int32, (KEY_BLOCK, rows), 0) - lax.broadcasted_iota(
        jnp.int32, (KEY_BLOCK, rows), 1
    )
    for head in range(group):
        absorbed = over_first(ka_ref[head], q_ref[head, :NOPE, :])
        qf_ref[head, :LATENT, :] = (absorbed * factor).astype(jnp.bfloat16)
        qf_ref[head, LATENT:, :] = (q_ref[head, NOPE:, :].astype(jnp.float32) * factor).astype(
            jnp.bfloat16
        )

    highest = None
    for step in range(group + 1):
        top = jnp.full((8, rows), -1e30, jnp.float32)
        total = jnp.zeros((8, rows), jnp.float32)
        mixed = jnp.zeros((LATENT, rows), jnp.float32)
        for begin in range(0, keys, KEY_BLOCK):
            block = pl.ds(begin, KEY_BLOCK)
            if step < group:
                scores = jnp.dot(
                    lat_ref[block, :], qf_ref[step], preferred_element_type=jnp.float32
                )
                scores = jnp.where(ahead <= query_start - begin, scores, -1e30)
                slots[step % 2][block, :] = scores
                top = jnp.maximum(top, jnp.max(scores.reshape(KEY_BLOCK // 8, 8, rows), axis=0))
            if step > 0:
                weights = jnp.exp2(slots[(step - 1) % 2][block, :] - highest)
                total = total + jnp.sum(weights.reshape(KEY_BLOCK // 8, 8, rows), axis=0)
                mixed = mixed + jnp.dot(
                    latt_ref[:LATENT, block],
                    weights.astype(jnp.bfloat16),
                    preferred_element_type=jnp.float32,
                )
        if step > 0:
            inverse = 1.0 / jnp.sum(total, axis=0, keepdims=True)
            out_ref[:, pl.ds((step - 1) * VHEAD, VHEAD)] = over_first(
                (mixed * inverse).astype(jnp.bfloat16), va_ref[step - 1]
            ).astype(jnp.bfloat16)
        highest = jnp.max(top, axis=0, keepdims=True)


def attention(first_head, count, query_start, queries_t, key_absorb, value_absorb, keys, keys_t):
    _, width, rows = queries_t.shape
    total, latent_width = keys.shape
    group = next(size for size in (4, 2, 1) if count % size == 0 and first_head % size == 0)
    first = first_head // group

    def by_head(i, _):
        return (first + i, 0, 0)

    return pl.pallas_call(
        attention_kernel,
        grid_spec=pltpu.PrefetchScalarGridSpec(
            num_scalar_prefetch=1,
            grid=(count // group,),
            in_specs=[
                pl.BlockSpec((group, width, rows), by_head),
                pl.BlockSpec((group, NOPE, LATENT), by_head),
                pl.BlockSpec((group, LATENT, VHEAD), by_head),
                pl.BlockSpec((total, latent_width), lambda i, _: (0, 0)),
                pl.BlockSpec((latent_width, total), lambda i, _: (0, 0)),
            ],
            out_specs=pl.BlockSpec((rows, group * VHEAD), lambda i, _: (0, i)),
            scratch_shapes=[
                pltpu.VMEM((group, latent_width, rows), jnp.bfloat16),
                pltpu.VMEM((total, rows), jnp.float32),
                pltpu.VMEM((total, rows), jnp.float32),
            ],
        ),
        out_shape=jax.ShapeDtypeStruct((rows, count * VHEAD), jnp.bfloat16),
        compiler_params=pltpu.CompilerParams(vmem_limit_bytes=50 * 2 ** 20),
        cost_estimate=pl.CostEstimate(
            flops=4 * count * rows * total * (latent_width + LATENT),
            bytes_accessed=count * (rows * 320 + 2 * NOPE * LATENT) * 2 + 4 * total * latent_width,
            transcendentals=count * rows * total,
        ),
    )(query_start, queries_t, key_absorb, value_absorb, keys, keys_t)


def join_kernel(count, *refs):
    begin = 0
    for place in range(count):
        width = refs[place].shape[1]
        refs[-1][:, pl.ds(begin, width)] = refs[place][...]
        begin += width


def join(pieces, after):
    rows = pieces[0].shape[0]
    width = sum(piece.shape[1] for piece in pieces)
    later = [] if after is None else [after]
    return pl.pallas_call(
        functools.partial(join_kernel, len(pieces)),
        in_specs=[pl.BlockSpec(memory_space=pltpu.VMEM)] * len(pieces)
        + [pl.BlockSpec(memory_space=pl.ANY)] * len(later),
        out_specs=pl.BlockSpec(memory_space=pltpu.VMEM),
        out_shape=jax.ShapeDtypeStruct((rows, width), jnp.bfloat16),
    )(*pieces, *later)


def project_kernel(added, source_ref, *refs):
    rows_ref, weight_ref, out_ref, sum_ref = refs[added:]
    step = pl.program_id(0)
    product = jnp.dot(rows_ref[...], weight_ref[...], preferred_element_type=jnp.float32)

    @pl.when(step == 0)
    def _():
        sum_ref[...] = product + refs[0][...] if added else product

    @pl.when(step > 0)
    def _():
        sum_ref[...] += product

    @pl.when(step == pl.num_programs(0) - 1)
    def _():
        out_ref[...] = sum_ref[...].astype(out_ref.dtype)


def project(so_far, gathered, out_proj, blocks, depth, held_as):
    rows, columns = gathered.shape[0], out_proj.shape[1]
    added = so_far is not None
    whole = pl.BlockSpec((rows, columns), lambda i, _: (0, 0))
    return pl.pallas_call(
        functools.partial(project_kernel, int(added)),
        grid_spec=pltpu.PrefetchScalarGridSpec(
            num_scalar_prefetch=1,
            grid=(gathered.shape[1] // depth,),
            in_specs=[whole] * added
            + [
                pl.BlockSpec((rows, depth), lambda i, _: (0, i)),
                pl.BlockSpec((depth, columns), lambda i, blocks: (blocks[i], 0)),
            ],
            out_specs=whole,
            scratch_shapes=[pltpu.VMEM((rows, columns), jnp.float32)],
        ),
        out_shape=jax.ShapeDtypeStruct((rows, columns), held_as),
        compiler_params=pltpu.CompilerParams(vmem_limit_bytes=56 * 2 ** 20),
        cost_estimate=pl.CostEstimate(
            flops=2 * rows * gathered.shape[1] * columns,
            bytes_accessed=2 * gathered.shape[1] * (rows + columns) + 8 * rows * columns,
            transcendentals=0,
        ),
    )(blocks, *([so_far] * added), gathered, out_proj)


def on_device(
    queries,
    latents,
    key_absorb,
    value_absorb,
    out_proj,
    residual_in,
    norm_gain,
    expert_gate,
    expert_up,
    expert_down,
    route_ids,
    route_weights,
):
    rows = queries.shape[0]
    local_heads = queries.shape[1]
    columns = out_proj.shape[1]
    ctx_count = lax.axis_size("ctx")
    ep_count = lax.axis_size("ep")
    ep_me = lax.axis_index("ep")
    owned = rows // ep_count
    query_start = (lax.axis_index("ctx") * rows).astype(jnp.int32).reshape(1)

    keys = lax.all_gather(latents, "ctx", axis=0, tiled=True)
    keys_t = keys.T
    queries_t = jnp.transpose(queries, (1, 2, 0))

    unit = local_heads // 8
    depth = unit * VHEAD
    heads, starts = [], []
    for part in EIGHTHS:
        starts.append(sum(EIGHTHS[: len(starts)]))
        heads.append(
            attention(
                starts[-1] * unit,
                part * unit,
                query_start,
                queries_t,
                key_absorb,
                value_absorb,
                keys,
                keys_t,
            )
        )
    complete = None
    for members, after in (((0,), heads[1]), ((1, 2), None)):
        pieces, blocks = [], []
        for member in members:
            for shift in range(ep_count):
                target = lax.rem(ep_me + shift, ep_count)
                source = lax.rem(ep_me - shift + ep_count, ep_count)
                block = lax.dynamic_slice_in_dim(heads[member], target * owned, owned, axis=0)
                if shift > 0:
                    block = lax.ppermute(
                        block, "ep", [(i, (i + shift) % ep_count) for i in range(ep_count)]
                    )
                pieces.append(block)
                for at in range(EIGHTHS[member]):
                    blocks.append(source * 8 + starts[member] + at)
        gathered = lax.all_gather(join(pieces, after), "ctx", axis=0, tiled=True)
        complete = project(
            complete,
            gathered,
            out_proj,
            jnp.stack(blocks).astype(jnp.int32),
            depth,
            jnp.float32 if complete is None else jnp.bfloat16,
        )
    complete = complete.reshape(ctx_count, -1, columns)
    attended = lax.all_to_all(complete, "ctx", split_axis=0, concat_axis=2, tiled=True).reshape(
        -1, columns * ctx_count
    )
    wide = residual_in.astype(jnp.float32) + attended.astype(jnp.float32)
    hidden = wide.astype(jnp.bfloat16)
    hidden_wide = hidden.astype(jnp.float32)
    square = jnp.mean(hidden_wide * hidden_wide, axis=1, keepdims=True)
    normed = (hidden_wide * lax.rsqrt(square + 1e-06) * norm_gain).astype(jnp.bfloat16)
    tokens_here = hidden.shape[0]
    window = ep_count
    flat_ids = route_ids.reshape(-1)
    chosen = (flat_ids[:, None] == jnp.arange(window, dtype=jnp.int32)[None, :]).astype(jnp.int32)
    earlier = jnp.cumsum(chosen, axis=0) - chosen
    slot = jnp.sum(earlier * chosen, axis=1)
    place = chosen[:, :, None] * (
        slot[:, None, None] == jnp.arange(CAP, dtype=jnp.int32)[None, None, :]
    ).astype(jnp.int32)
    place = place.reshape(tokens_here, TOPK, window * CAP).astype(jnp.float32)
    gather_table = jnp.sum(place, axis=1).astype(jnp.bfloat16)
    combine_table = jnp.sum(place * route_weights[:, :, None], axis=1)
    outgoing = lax.dot_general(
        gather_table, normed, (((0,), (0,)), ((), ())), preferred_element_type=jnp.float32
    ).astype(jnp.bfloat16)
    outgoing = outgoing.reshape(window, CAP, -1)
    arrived = lax.all_to_all(outgoing, "ep", split_axis=0, concat_axis=0, tiled=True)
    gate_weight = expert_gate[0]
    up_weight = expert_up[0]
    down_weight = expert_down[0]

    flat_rows = lax.all_gather(arrived, "ctx", axis=0, tiled=True).reshape(
        ctx_count * window * CAP, -1
    )
    gate = jnp.dot(flat_rows, gate_weight, preferred_element_type=jnp.float32)
    upper = jnp.dot(flat_rows, up_weight, preferred_element_type=jnp.float32)
    activated = (jax.nn.silu(gate) * upper).astype(jnp.bfloat16)
    partial_out = jnp.dot(activated, down_weight, preferred_element_type=jnp.float32)
    partial_out = partial_out.astype(jnp.bfloat16).reshape(ctx_count, window * CAP, -1)
    parts = lax.all_to_all(partial_out, "ctx", split_axis=0, concat_axis=0, tiled=True)
    result = jnp.sum(parts.astype(jnp.float32), axis=0).astype(jnp.bfloat16)
    result = result.reshape(window, CAP, -1)
    returned = lax.all_to_all(result, "ep", split_axis=0, concat_axis=0, tiled=True)
    mixture = jnp.dot(
        combine_table,
        returned.reshape(window * CAP, -1).astype(jnp.float32),
        precision=lax.Precision.HIGHEST,
    )
    return (hidden_wide + mixture).astype(jnp.bfloat16)


def solution(mesh):
    placed = (
        P("ctx", "ep", None),
        P("ctx", None),
        P("ep", None, None),
        P("ep", None, None),
        P(None, "ctx"),
        P(("ctx", "ep"), None),
        P(),
        P("ep", None, "ctx"),
        P("ep", None, "ctx"),
        P("ep", "ctx", None),
        P(("ctx", "ep"), None),
        P(("ctx", "ep"), None),
    )
    return jax.shard_map(
        on_device, mesh=mesh, in_specs=placed, out_specs=P(("ctx", "ep"), None), check_vma=False
    )
```
